32 devices in a mesh: row: 2 (over core), col: 4 (over z), cell: 4 (over y, x).
Axes of the slice: x: 2, y: 2, z: 4, core: 2. Of those that a mesh axis runs over, the one named last changes fastest.
Arguments:
- populations: float32 [16384, 1024], P(('row', 'col'), 'cell'), parts along dimension 1, may hold values from -6 to 6
- source: float32 [16384, 1024], P(('row', 'col'), 'cell'), parts along dimension 1, may hold values from -6 to 6
- loss_rates: float32 [8, 16384], P(None, ('row', 'col')), may hold values from 0.05 to 0.5
- basis_table: float32 [8, 64], replicated, may hold values from 0.25 to 4
- temp_bins: int32 [1024], P('cell'), parts along dimension 0, may hold values from 0 to 63
- rate_blocks: bfloat16 [2, 4, 32, 8, 128, 128], P('row', 'col'), may hold values from -0.09375 to 0.09375
- block_rows: int32 [2, 4, 32], P('row', 'col'), may hold values from 0 to 31, as said below
- block_cols: int32 [2, 4, 32], P('row', 'col'), may hold values from 0 to 63, as said below
- block_count: int32 [2, 4], P('row', 'col'), may hold values from 1 to 32, as said below
Outputs:
- updated: float32 [16384, 1024], P(('row', 'col'), 'cell'), parts along dimension 1
The draws below stay inside these ranges and needn't reach their ends.
There are 4 independent parts, one for each index of `cell`. The reference program is written for one: setup_inputs(seed, part) draws one part's arguments, and reference() takes and returns one part's arrays. A program takes and returns all parts, laid end to end along the dimension named above; an argument that names none is the same for every part. Nothing has to cross between parts.
Inputs may be any that keep to these rules, and one draw needn't show every extreme that they name: The slots of a tile name distinct block positions (block_rows, block_cols); every tile names its first and its last block position among its slots. `block_cols`: paired with block_rows slot by slot. `block_count`: in one index of row, drawn from the seed, every tile has 32 live slots; every other tile has at most 16.
All inputs are finite; a program needn't handle non-finite values.
Results may differ from the reference program's by a relative error of at most 0.002.
Values sent between devices are 32-bit elements; how exact they have to be, the bound alone decides.
A program may use at most 128 MiB of HBM per device.

```python
import math
import jax
import jax.numpy as jnp
from jax import lax

LEVELS = 16384
BLOCK = 128
BASIS = 8
BINS = 64
ITERS = 2
CELLS = 256
CAP = 32
PIECE = 2048
TILE_ROWS = 32
TILE_COLS = 64
N_ROW = 2
N_COL = 4


def slot_positions(key):
    base = jax.random.fold_in(key, 17)
    spots = TILE_ROWS * TILE_COLS
    tile_keys = jax.random.split(base, N_ROW * N_COL)

    def one_tile(tile_key):
        first_key, second_key = jax.random.split(tile_key)
        middle = (jax.random.permutation(first_key, spots - 2) + 1).astype(jnp.int32)
        listed = jnp.concatenate([jnp.array([0, spots - 1], dtype=jnp.int32), middle])[:CAP]
        ordering = jax.random.permutation(second_key, CAP)
        return listed[ordering]
    return jax.vmap(one_tile)(tile_keys).reshape(N_ROW, N_COL, CAP).astype(jnp.int32)


def draw_block_rows(key, part):
    return (slot_positions(key) // TILE_COLS).astype(jnp.int32)


def draw_block_cols(key, part):
    return (slot_positions(key) % TILE_COLS).astype(jnp.int32)


def draw_block_count(key, part):
    base = jax.random.fold_in(key, 29)
    first_key, second_key = jax.random.split(base)
    light = jax.random.randint(first_key, (N_ROW, N_COL), 1, CAP // 2 + 1)
    hot_row = jax.random.randint(second_key, (), 0, N_ROW)
    ranks = lax.broadcasted_iota(jnp.int32, (N_ROW, N_COL), 0)
    return jnp.where(ranks == hot_row, CAP, light).astype(jnp.int32)


def with_ends(entries, key, low, largest):
    index_at = [jax.random.randint(jax.random.fold_in(key, axis), (), 0, length) for axis, length in enumerate(entries.shape)]
    longest = entries.shape.index(max(entries.shape))
    next_to = index_at[:longest] + [(index_at[longest] + 1) % entries.shape[longest]] + index_at[longest + 1:]
    return entries.at[tuple(index_at)].set(low).at[tuple(next_to)].set(largest)


def block_levels(stream_key, shape, pieces, low, high):
    def one(dim, parts):
        draws = jax.random.uniform(jax.random.fold_in(jax.random.fold_in(stream_key, 6), dim), (parts,), jnp.float32, low / len(pieces), high / len(pieces))
        return jnp.repeat(jnp.exp(draws), shape[dim] // parts).reshape((-1,) + (1,) * (len(shape) - dim - 1))

    level = one(*pieces[0])
    for cut in pieces[1:]:
        level = level * one(*cut)
    return level


def normal_values(own_key, dims, scale, most, shards=(), held_as=jnp.bfloat16):
    entries = jax.random.normal(own_key, dims, jnp.float32) * scale
    if len(shards) > 0:
        entries = block_levels(own_key, dims, shards, -0.22, 0.18) * entries
    return jnp.clip(entries, min=-most, max=most).astype(held_as)


def setup_inputs(seed: int = 0, part: int = 0) -> dict:
    seeds = jax.random.split(jax.random.key(seed), 10)
    own_keys = jax.random.split(jax.random.fold_in(seeds[9], part), 10)
    return {
        "populations": normal_values(own_keys[0], (LEVELS, CELLS), 1.0, 6.0, ((0, 8),), jnp.float32),
        "source": normal_values(own_keys[1], (LEVELS, CELLS), 1.0, 6.0, ((0, 8),), jnp.float32),
        "loss_rates": jnp.clip(jnp.exp(math.log(0.5) - 2.3025851 * jax.random.uniform(seeds[2], (BASIS, LEVELS), jnp.float32) ** block_levels(seeds[2], (BASIS, LEVELS), ((1, 8),), -0.2, 0.2)), 0.05, 0.5),
        "basis_table": jnp.clip(jnp.exp(jax.random.uniform(seeds[3], (BASIS, BINS), jnp.float32, math.log(0.25), math.log(4.0))), 0.25, 4.0),
        "temp_bins": with_ends(jax.random.randint(own_keys[4], (CELLS,), 0, BINS), jax.random.fold_in(own_keys[4], 1), 0, BINS - 1).astype(jnp.int32),
        "rate_blocks": normal_values(seeds[5], (N_ROW, N_COL, CAP, BASIS, BLOCK, BLOCK), (4 * BLOCK * BASIS) ** -0.5, 0.09375, ((0, 2), (1, 4))),
        "block_rows": draw_block_rows(jax.random.fold_in(seeds[9], 71), part),
        "block_cols": draw_block_cols(jax.random.fold_in(seeds[9], 71), part),
        "block_count": draw_block_count(jax.random.fold_in(seeds[9], 71), part),
    }


def reference(populations, source, loss_rates, basis_table, temp_bins, rate_blocks, block_rows, block_cols, block_count):
    onehot = (temp_bins[None, :] == jnp.arange(BINS, dtype=jnp.int32)[:, None]).astype(jnp.float32)
    factors = jnp.dot(basis_table, onehot, precision=lax.Precision.HIGHEST)
    denominator = jnp.einsum("kl,kc->lc", loss_rates, factors, precision=lax.Precision.HIGHEST)
    per_piece = PIECE // BLOCK
    tile_row = lax.broadcasted_iota(jnp.int32, (N_ROW, N_COL, CAP), 0)
    tile_col = lax.broadcasted_iota(jnp.int32, (N_ROW, N_COL, CAP), 1)
    slot_index = lax.broadcasted_iota(jnp.int32, (N_ROW, N_COL, CAP), 2)
    global_rows = (((block_rows // per_piece) * N_COL + tile_col) * per_piece + block_rows % per_piece).reshape(-1).astype(jnp.int32)
    global_cols = (tile_row * (N_COL * per_piece) + block_cols).reshape(-1).astype(jnp.int32)
    live_mask = (slot_index < block_count[:, :, None]).astype(jnp.float32).reshape(-1)
    slot_total = N_ROW * N_COL * CAP
    flat_blocks = rate_blocks.reshape(slot_total, BASIS, BLOCK, BLOCK)
    for sweep in range(ITERS):
        weighted = (factors[:, None, :] * populations[None, :, :]).astype(jnp.bfloat16)

        def add_slot(slot, totals):
            block_data = lax.dynamic_index_in_dim(flat_blocks, slot, 0, keepdims=False).astype(jnp.float32)
            col_start = (global_cols[slot] * BLOCK).astype(jnp.int32)
            columns = lax.dynamic_slice_in_dim(weighted, col_start, BLOCK, 1).astype(jnp.float32)
            product = jnp.einsum("kij,kjc->ic", block_data, columns) * live_mask[slot]
            row_start = (global_rows[slot] * BLOCK).astype(jnp.int32)
            current = lax.dynamic_slice_in_dim(totals, row_start, BLOCK, 0)
            return lax.dynamic_update_slice_in_dim(totals, current + product, row_start, 0)

        coupling = lax.fori_loop(0, slot_total, add_slot, jnp.zeros((LEVELS, CELLS), jnp.float32))
        populations = (source + coupling) / denominator
    return populations
```

```python
import jax
import jax.numpy as jnp
from jax import lax
from jax.experimental import pallas as pl
from jax.experimental.pallas import tpu as pltpu
from jax.sharding import PartitionSpec as P

ITERS = 2


def slots_kernel(count_ref, cols_ref, dest_ref, rates_ref, held_ref, factors_ref, theirs_ref, mine_ref):
    basis = rates_ref.shape[1]
    depth = mine_ref.shape[0]
    theirs_ref[...] = jnp.zeros_like(theirs_ref)
    mine_ref[...] = jnp.zeros_like(mine_ref)

    def slot_step(slot, carry):
        block = held_ref[cols_ref[slot]]
        weighted = jnp.concatenate(
            [(factors_ref[k : k + 1, :] * block).astype(jnp.bfloat16) for k in range(basis)], axis=0
        )
        rates = jnp.concatenate([rates_ref[slot, k] for k in range(basis)], axis=1)
        product = jnp.dot(rates, weighted, preferred_element_type=jnp.float32)
        place = dest_ref[slot]

        @pl.when(place < depth)
        def _():
            mine_ref[place] += product

        @pl.when(place >= depth)
        def _():
            theirs_ref[place - depth] += product

        return carry

    lax.fori_loop(0, count_ref[0], slot_step, 0)


def slot_sums(count, cols, dest, rates, held, factors, depth):
    slots, basis, block, _ = rates.shape
    cells = factors.shape[1]
    smem = pl.BlockSpec(memory_space=pltpu.SMEM)
    vmem = pl.BlockSpec(memory_space=pltpu.VMEM)
    half = jax.ShapeDtypeStruct((depth, block, cells), jnp.float32)
    return pl.pallas_call(
        slots_kernel,
        out_shape=(half, half),
        in_specs=[smem, smem, smem, vmem, vmem, vmem],
        out_specs=(vmem, vmem),
        compiler_params=pltpu.CompilerParams(vmem_limit_bytes=40 * 1024 * 1024),
        cost_estimate=pl.CostEstimate(
            flops=2 * slots * basis * block * block * cells,
            bytes_accessed=rates.size * 2 + held.size * 4 + 2 * depth * block * cells * 4,
            transcendentals=0,
        ),
    )(count, cols, dest, rates, held, factors)


def per_device(
    populations,
    source,
    loss_rates,
    basis_table,
    temp_bins,
    rate_blocks,
    block_rows,
    block_cols,
    block_count,
):
    levels, cells = populations.shape
    bin_count = basis_table.shape[1]
    block = rate_blocks.shape[-1]
    per_piece = levels // block
    onehot = (temp_bins[None, :] == jnp.arange(bin_count, dtype=jnp.int32)[:, None]).astype(
        jnp.float32
    )
    factors = jnp.dot(basis_table, onehot, precision=lax.Precision.HIGHEST)
    denominator = jnp.einsum("kl,kc->lc", loss_rates, factors, precision=lax.Precision.HIGHEST)
    rates = rate_blocks[0, 0]
    rows = block_rows[0, 0]
    own = rows // per_piece == lax.axis_index("row")
    dest = rows % per_piece + jnp.where(own, 0, per_piece)
    for sweep in range(ITERS):
        held = lax.all_gather(populations, "col", axis=0, tiled=True).reshape(-1, block, cells)
        theirs, mine = slot_sums(
            block_count[0], block_cols[0, 0], dest, rates, held, factors, per_piece
        )
        arrived = lax.ppermute(theirs, "row", [(0, 1), (1, 0)])
        coupling = (mine + arrived).reshape(levels, cells)
        populations = (source + coupling) / denominator
    return populations


def solution(mesh):
    in_specs = (
        P(("row", "col"), "cell"),
        P(("row", "col"), "cell"),
        P(None, ("row", "col")),
        P(),
        P("cell"),
        P("row", "col", None, None, None, None),
        P("row", "col", None),
        P("row", "col", None),
        P("row", "col"),
    )
    out_specs = P(("row", "col"), "cell")
    return jax.shard_map(
        per_device, mesh=mesh, in_specs=in_specs, out_specs=out_specs, check_vma=False
    )
```

```python
import functools

import jax
import jax.numpy as jnp
from jax import lax
from jax.experimental import pallas as pl
from jax.experimental.pallas import tpu as pltpu
from jax.sharding import PartitionSpec as P

ITERS = 2


MESH = pl.DeviceIdType.MESH
CAPACITIES = ((9, 5), (10, 6), (12, 8))


def pick_kernel(n, capacities, picks_ref, held_ref, got_ref, packed, send_sem, recv_sem):
    me = lax.axis_index("col")
    row = lax.axis_index("row")
    depth = held_ref.shape[0]
    barrier = pltpu.get_barrier_semaphore()
    for far in range(1, n):
        peer = lax.rem(me + far, n)
        pl.semaphore_signal(barrier, inc=1, device_id={"col": peer}, device_id_type=MESH)
    pl.semaphore_wait(barrier, n - 1)

    def exchange(capacity):
        copies = []
        for far in sorted(range(1, n), key=lambda far: abs(2 * far - n)):

            def pack(k, carry):
                packed[far - 1, k] = held_ref[picks_ref[(far - 1) * depth + k]]
                return carry

            lax.fori_loop(0, capacity, pack, 0)
            copy = pltpu.make_async_remote_copy(
                src_ref=packed.at[far - 1, pl.ds(0, capacity)],
                dst_ref=got_ref.at[far - 1, pl.ds(0, capacity)],
                send_sem=send_sem.at[far - 1],
                recv_sem=recv_sem.at[far - 1],
                device_id={"col": lax.rem(me + far, n)},
                device_id_type=MESH,
            )
            copy.start()
            copies.append(copy)
        for copy in copies:
            copy.wait()

    for index, capacity in enumerate(capacities):
        pl.when(row == index)(functools.partial(exchange, capacity))


def picked_blocks(n, capacities, collective, picks, held):
    most = max(capacities)
    depth, block, cells = held.shape
    shape = (n - 1, most, block, cells)
    return pl.pallas_call(
        functools.partial(pick_kernel, n, capacities),
        out_shape=jax.ShapeDtypeStruct(shape, jnp.float32),
        in_specs=[
            pl.BlockSpec(memory_space=pltpu.SMEM),
            pl.BlockSpec(memory_space=pltpu.VMEM),
        ],
        out_specs=pl.BlockSpec(memory_space=pl.ANY),
        scratch_shapes=[
            pltpu.VMEM(shape, jnp.float32),
            pltpu.SemaphoreType.DMA((n - 1,)),
            pltpu.SemaphoreType.DMA((n - 1,)),
        ],
        compiler_params=pltpu.CompilerParams(
            collective_id=collective,
            has_side_effects=True,
            vmem_limit_bytes=24 * 1024 * 1024,
        ),
        cost_estimate=pl.CostEstimate(
            flops=0, bytes_accessed=4 * (n - 1) * most * block * cells * 4, transcendentals=0
        ),
    )(picks, held)


def slots_kernel(
    count_ref, cols_ref, dest_ref, rates_ref, near_ref, far_ref, factors_ref, theirs_ref, mine_ref
):
    basis = rates_ref.shape[1]
    depth = mine_ref.shape[0]
    near = near_ref.shape[0]
    theirs_ref[...] = jnp.zeros_like(theirs_ref)
    mine_ref[...] = jnp.zeros_like(mine_ref)

    def add_product(slot, block):
        weighted = jnp.concatenate(
            [(factors_ref[k : k + 1, :] * block).astype(jnp.bfloat16) for k in range(basis)], axis=0
        )
        rates = jnp.concatenate([rates_ref[slot, k] for k in range(basis)], axis=1)
        product = jnp.dot(rates, weighted, preferred_element_type=jnp.float32)
        place = dest_ref[slot]

        @pl.when(place < depth)
        def _():
            mine_ref[place] += product

        @pl.when(place >= depth)
        def _():
            theirs_ref[place - depth] += product

    def slot_step(slot, carry):
        column = cols_ref[slot]

        @pl.when(column < near)
        def _():
            add_product(slot, near_ref[column])

        @pl.when(column >= near)
        def _():
            add_product(slot, far_ref[column - near])

        return carry

    lax.fori_loop(0, count_ref[0], slot_step, 0)


def slot_sums(count, cols, dest, rates, near, far, factors):
    slots, basis, block, _ = rates.shape
    depth, _, cells = near.shape
    smem = pl.BlockSpec(memory_space=pltpu.SMEM)
    vmem = pl.BlockSpec(memory_space=pltpu.VMEM)
    half = jax.ShapeDtypeStruct((depth, block, cells), jnp.float32)
    return pl.pallas_call(
        slots_kernel,
        out_shape=(half, half),
        in_specs=[smem, smem, smem, vmem, vmem, vmem, vmem],
        out_specs=(vmem, vmem),
        compiler_params=pltpu.CompilerParams(vmem_limit_bytes=40 * 1024 * 1024),
        cost_estimate=pl.CostEstimate(
            flops=2 * slots * basis * block * block * cells,
            bytes_accessed=rates.size * 2 + far.size * 4 + 3 * depth * block * cells * 4,
            transcendentals=0,
        ),
    )(count, cols, dest, rates, near, far, factors)


def per_device(
    populations,
    source,
    loss_rates,
    basis_table,
    temp_bins,
    rate_blocks,
    block_rows,
    block_cols,
    block_count,
):
    levels, cells = populations.shape
    bin_count = basis_table.shape[1]
    block = rate_blocks.shape[-1]
    slots = rate_blocks.shape[2]
    per_piece = levels // block
    n = lax.axis_size("col")
    tile_rows = lax.axis_size("row")
    row, me = lax.axis_index("row"), lax.axis_index("col")
    onehot = (temp_bins[None, :] == jnp.arange(bin_count, dtype=jnp.int32)[:, None]).astype(
        jnp.float32
    )
    factors = jnp.dot(basis_table, onehot, precision=lax.Precision.HIGHEST)
    denominator = jnp.einsum("kl,kc->lc", loss_rates, factors, precision=lax.Precision.HIGHEST)
    denominator = denominator.reshape(per_piece, block, cells)
    source = source.reshape(per_piece, block, cells)
    rates = rate_blocks[0, 0]
    rows, cols, count = block_rows[0, 0], block_cols[0, 0], block_count[0]
    own = rows // per_piece == row
    dest = rows % per_piece + jnp.where(own, 0, per_piece)

    def sweeps(columns, gather):
        held = populations.reshape(per_piece, block, cells)
        for sweep in range(ITERS):
            theirs, mine = slot_sums(count, columns, dest, rates, held, gather(held), factors)
            arrived = lax.ppermute(theirs, "row", [(0, 1), (1, 0)])
            held = (source + (mine + arrived)) / denominator
        return held.reshape(levels, cells)

    def whole():
        return sweeps(
            cols + per_piece, lambda held: lax.all_gather(held, "col", axis=0, tiled=True)
        )

    pairs = []
    for high, low in CAPACITIES:
        if high < per_piece:
            pairs += [(high, low), (low, high)]
    if not pairs:
        return whole()

    live = jnp.arange(slots, dtype=jnp.int32) < count[0]
    spots = jnp.arange(n * per_piece, dtype=jnp.int32)
    named = jnp.any((cols[None, :] == spots[:, None]) & live[None, :], axis=1).astype(jnp.int32)
    every = lax.all_gather(named, ("row", "col"), axis=0)
    every = every.reshape(tile_rows, n, n, per_piece)
    apart = 1 - jnp.eye(n, dtype=jnp.int32)
    needed = jnp.max(jnp.sum(every, axis=3) * apart[None], axis=(1, 2))

    ranks = jnp.arange(per_piece, dtype=jnp.int32)
    below = (ranks[:, None] < ranks[None, :]).astype(jnp.int32)

    def order(mask):
        return jnp.sum(mask[..., :, None] * below, axis=-2)

    asked = lax.dynamic_index_in_dim(
        lax.dynamic_index_in_dim(every, row, 0, False), me, 1, False
    )
    at = order(asked)
    chosen = (at[:, :, None] == ranks[None, None, :]) & (asked[:, :, None] > 0)
    lists = jnp.sum(jnp.where(chosen, ranks[None, :, None], 0), axis=1)
    readers = (me + jnp.arange(1, n, dtype=jnp.int32)) % n
    picks = jnp.sum(
        jnp.where((readers[:, None] == jnp.arange(n)[None, :])[:, :, None], lists[None], 0), axis=1
    ).reshape(-1)

    places = order(named.reshape(n, per_piece)).reshape(-1)
    place = jnp.sum(jnp.where(cols[None, :] == spots[:, None], places[:, None], 0), axis=0)
    back = (me - cols // per_piece + n) % n

    def sparse(index, capacities):
        most = max(capacities)
        columns = jnp.where(
            back == 0, cols % per_piece, per_piece + (back - 1) * most + place
        ).astype(jnp.int32)

        def gather(held):
            got = picked_blocks(n, capacities, index, picks, held)
            return got.reshape((n - 1) * most, block, cells)

        return lambda: sweeps(columns, gather)

    fits = jnp.stack(
        [jnp.all(needed <= jnp.asarray(pair, jnp.int32)) for pair in pairs] + [jnp.bool_(True)]
    )
    branch = jnp.argmax(fits).astype(jnp.int32)
    return lax.switch(branch, [sparse(i, pair) for i, pair in enumerate(pairs)] + [whole])


def solution(mesh):
    in_specs = (
        P(("row", "col"), "cell"),
        P(("row", "col"), "cell"),
        P(None, ("row", "col")),
        P(),
        P("cell"),
        P("row", "col", None, None, None, None),
        P("row", "col", None),
        P("row", "col", None),
        P("row", "col"),
    )
    out_specs = P(("row", "col"), "cell")
    return jax.shard_map(
        per_device, mesh=mesh, in_specs=in_specs, out_specs=out_specs, check_vma=False
    )
```

```python
import functools

import jax
import jax.numpy as jnp
from jax import lax
from jax.experimental import pallas as pl
from jax.experimental.pallas import tpu as pltpu
from jax.sharding import PartitionSpec as P

ITERS = 2


MESH = pl.DeviceIdType.MESH
CAPACITIES = ((8, 4), (9, 5), (10, 5), (10, 6), (12, 8))


def pick_kernel(n, capacities, picks_ref, held_ref, got_ref, packed, passing, send_sem, recv_sem):
    me = lax.axis_index("col")
    row = lax.axis_index("row")
    depth = held_ref.shape[0]
    barrier = pltpu.get_barrier_semaphore()
    for far in range(1, n):
        peer = lax.rem(me + far, n)
        pl.semaphore_signal(barrier, inc=1, device_id={"col": peer}, device_id_type=MESH)
    pl.semaphore_wait(barrier, n - 1)

    def send(source, target, far, sem):
        copy = pltpu.make_async_remote_copy(
            src_ref=source,
            dst_ref=target,
            send_sem=send_sem.at[sem],
            recv_sem=recv_sem.at[sem],
            device_id={"col": lax.rem(me + far, n)},
            device_id_type=MESH,
        )
        copy.start()
        return copy

    def exchange(capacity):
        copies = []
        onward = None
        for far in sorted(range(1, n), key=lambda far: (abs(2 * far - n), -far)):

            def pack(k, carry):
                packed[far - 1, k] = held_ref[picks_ref[(far - 1) * depth + k]]
                return carry

            lax.fori_loop(0, capacity, pack, 0)
            turned = capacity // 2 if n == 4 and far == 2 else 0
            straight = pl.ds(0, capacity - turned)
            if turned:
                rest = pl.ds(capacity - turned, turned)
                onward = (pl.ds(0, turned), rest)
                first = send(packed.at[1, rest], passing.at[onward[0]], n - 1, n - 1)
            copies.append(
                send(packed.at[far - 1, straight], got_ref.at[far - 1, straight], far, far - 1)
            )
        if onward:
            first.wait_recv()
            copies.append(send(passing.at[onward[0]], got_ref.at[1, onward[1]], n - 1, n))
            first.wait_send()
        for copy in copies:
            copy.wait()

    for index, capacity in enumerate(capacities):
        pl.when(row == index)(functools.partial(exchange, capacity))


def picked_blocks(n, capacities, collective, picks, held):
    most = max(capacities)
    depth, block, cells = held.shape
    shape = (n - 1, most, block, cells)
    return pl.pallas_call(
        functools.partial(pick_kernel, n, capacities),
        out_shape=jax.ShapeDtypeStruct(shape, jnp.float32),
        in_specs=[
            pl.BlockSpec(memory_space=pltpu.SMEM),
            pl.BlockSpec(memory_space=pltpu.VMEM),
        ],
        out_specs=pl.BlockSpec(memory_space=pl.ANY),
        scratch_shapes=[
            pltpu.VMEM(shape, jnp.float32),
            pltpu.VMEM(((most + 1) // 2, block, cells), jnp.float32),
            pltpu.SemaphoreType.DMA((n + 1,)),
            pltpu.SemaphoreType.DMA((n + 1,)),
        ],
        compiler_params=pltpu.CompilerParams(
            collective_id=collective,
            has_side_effects=True,
            vmem_limit_bytes=24 * 1024 * 1024,
        ),
        cost_estimate=pl.CostEstimate(
            flops=0, bytes_accessed=4 * (n - 1) * most * block * cells * 4, transcendentals=0
        ),
    )(picks, held)


def slots_kernel(
    count_ref, cols_ref, dest_ref, rates_ref, near_ref, far_ref, factors_ref, theirs_ref, mine_ref
):
    basis = rates_ref.shape[1]
    depth = mine_ref.shape[0]
    near = near_ref.shape[0]
    theirs_ref[...] = jnp.zeros_like(theirs_ref)
    mine_ref[...] = jnp.zeros_like(mine_ref)

    def add_product(slot, block):
        weighted = jnp.concatenate(
            [(factors_ref[k : k + 1, :] * block).astype(jnp.bfloat16) for k in range(basis)], axis=0
        )
        rates = jnp.concatenate([rates_ref[slot, k] for k in range(basis)], axis=1)
        product = jnp.dot(rates, weighted, preferred_element_type=jnp.float32)
        place = dest_ref[slot]

        @pl.when(place < depth)
        def _():
            mine_ref[place] += product

        @pl.when(place >= depth)
        def _():
            theirs_ref[place - depth] += product

    def slot_step(slot, carry):
        column = cols_ref[slot]

        @pl.when(column < near)
        def _():
            add_product(slot, near_ref[column])

        @pl.when(column >= near)
        def _():
            add_product(slot, far_ref[column - near])

        return carry

    lax.fori_loop(0, count_ref[0], slot_step, 0)


def slot_sums(count, cols, dest, rates, near, far, factors):
    slots, basis, block, _ = rates.shape
    depth, _, cells = near.shape
    smem = pl.BlockSpec(memory_space=pltpu.SMEM)
    vmem = pl.BlockSpec(memory_space=pltpu.VMEM)
    half = jax.ShapeDtypeStruct((depth, block, cells), jnp.float32)
    return pl.pallas_call(
        slots_kernel,
        out_shape=(half, half),
        in_specs=[smem, smem, smem, vmem, vmem, vmem, vmem],
        out_specs=(vmem, vmem),
        compiler_params=pltpu.CompilerParams(vmem_limit_bytes=40 * 1024 * 1024),
        cost_estimate=pl.CostEstimate(
            flops=2 * slots * basis * block * block * cells,
            bytes_accessed=rates.size * 2 + far.size * 4 + 3 * depth * block * cells * 4,
            transcendentals=0,
        ),
    )(count, cols, dest, rates, near, far, factors)


def per_device(
    populations,
    source,
    loss_rates,
    basis_table,
    temp_bins,
    rate_blocks,
    block_rows,
    block_cols,
    block_count,
):
    levels, cells = populations.shape
    bin_count = basis_table.shape[1]
    block = rate_blocks.shape[-1]
    slots = rate_blocks.shape[2]
    per_piece = levels // block
    n = lax.axis_size("col")
    tile_rows = lax.axis_size("row")
    row, me = lax.axis_index("row"), lax.axis_index("col")
    onehot = (temp_bins[None, :] == jnp.arange(bin_count, dtype=jnp.int32)[:, None]).astype(
        jnp.float32
    )
    factors = jnp.dot(basis_table, onehot, precision=lax.Precision.HIGHEST)
    denominator = jnp.einsum("kl,kc->lc", loss_rates, factors, precision=lax.Precision.HIGHEST)
    denominator = denominator.reshape(per_piece, block, cells)
    source = source.reshape(per_piece, block, cells)
    rates = rate_blocks[0, 0]
    rows, cols, count = block_rows[0, 0], block_cols[0, 0], block_count[0]
    own = rows // per_piece == row
    dest = rows % per_piece + jnp.where(own, 0, per_piece)

    def sweeps(columns, gather):
        held = populations.reshape(per_piece, block, cells)
        for sweep in range(ITERS):
            theirs, mine = slot_sums(count, columns, dest, rates, held, gather(held), factors)
            arrived = lax.ppermute(theirs, "row", [(0, 1), (1, 0)])
            held = (source + (mine + arrived)) / denominator
        return held.reshape(levels, cells)

    def whole():
        return sweeps(
            cols + per_piece, lambda held: lax.all_gather(held, "col", axis=0, tiled=True)
        )

    pairs = []
    for high, low in CAPACITIES:
        if high < per_piece:
            pairs += [(high, low), (low, high)]
    if not pairs:
        return whole()

    live = jnp.arange(slots, dtype=jnp.int32) < count[0]
    spots = jnp.arange(n * per_piece, dtype=jnp.int32)
    named = jnp.any((cols[None, :] == spots[:, None]) & live[None, :], axis=1).astype(jnp.int32)
    every = lax.all_gather(named, ("row", "col"), axis=0)
    every = every.reshape(tile_rows, n, n, per_piece)
    apart = 1 - jnp.eye(n, dtype=jnp.int32)
    needed = jnp.max(jnp.sum(every, axis=3) * apart[None], axis=(1, 2))

    ranks = jnp.arange(per_piece, dtype=jnp.int32)
    below = (ranks[:, None] < ranks[None, :]).astype(jnp.int32)

    def order(mask):
        return jnp.sum(mask[..., :, None] * below, axis=-2)

    asked = lax.dynamic_index_in_dim(
        lax.dynamic_index_in_dim(every, row, 0, False), me, 1, False
    )
    at = order(asked)
    chosen = (at[:, :, None] == ranks[None, None, :]) & (asked[:, :, None] > 0)
    lists = jnp.sum(jnp.where(chosen, ranks[None, :, None], 0), axis=1)
    readers = (me + jnp.arange(1, n, dtype=jnp.int32)) % n
    picks = jnp.sum(
        jnp.where((readers[:, None] == jnp.arange(n)[None, :])[:, :, None], lists[None], 0), axis=1
    ).reshape(-1)

    places = order(named.reshape(n, per_piece)).reshape(-1)
    place = jnp.sum(jnp.where(cols[None, :] == spots[:, None], places[:, None], 0), axis=0)
    back = (me - cols // per_piece + n) % n

    def sparse(index, capacities):
        most = max(capacities)
        columns = jnp.where(
            back == 0, cols % per_piece, per_piece + (back - 1) * most + place
        ).astype(jnp.int32)

        def gather(held):
            got = picked_blocks(n, capacities, index, picks, held)
            return got.reshape((n - 1) * most, block, cells)

        return lambda: sweeps(columns, gather)

    fits = jnp.stack(
        [jnp.all(needed <= jnp.asarray(pair, jnp.int32)) for pair in pairs] + [jnp.bool_(True)]
    )
    branch = jnp.argmax(fits).astype(jnp.int32)
    return lax.switch(branch, [sparse(i, pair) for i, pair in enumerate(pairs)] + [whole])


def solution(mesh):
    in_specs = (
        P(("row", "col"), "cell"),
        P(("row", "col"), "cell"),
        P(None, ("row", "col")),
        P(),
        P("cell"),
        P("row", "col", None, None, None, None),
        P("row", "col", None),
        P("row", "col", None),
        P("row", "col"),
    )
    out_specs = P(("row", "col"), "cell")
    return jax.shard_map(
        per_device, mesh=mesh, in_specs=in_specs, out_specs=out_specs, check_vma=False
    )
```

```python
import functools

import jax
import jax.numpy as jnp
from jax import lax
from jax.experimental import pallas as pl
from jax.experimental.pallas import tpu as pltpu
from jax.sharding import PartitionSpec as P

ITERS = 2


MESH = pl.DeviceIdType.MESH
CAPACITIES = ((8, 4), (9, 4), (9, 5), (10, 6), (12, 8))
EXTRA = 3


def pick_kernel(n, capacities, picks_ref, held_ref, got_ref, packed, send_sem, recv_sem):
    me = lax.axis_index("col")
    row = lax.axis_index("row")
    depth = held_ref.shape[0]
    barrier = pltpu.get_barrier_semaphore()
    for far in range(1, n):
        peer = lax.rem(me + far, n)
        pl.semaphore_signal(barrier, inc=1, device_id={"col": peer}, device_id_type=MESH)
    pl.semaphore_wait(barrier, n - 1)

    def half(device):
        return lax.div(2 * device, n)

    def exchange(capacity):
        wide = min(capacity + EXTRA, depth)
        order = sorted(range(1, n), key=lambda far: abs(2 * far - n))

        def copy(far, size):
            return pltpu.make_async_remote_copy(
                src_ref=packed.at[far - 1, pl.ds(0, size)],
                dst_ref=got_ref.at[far - 1, pl.ds(0, size)],
                send_sem=send_sem.at[far - 1],
                recv_sem=recv_sem.at[far - 1],
                device_id={"col": lax.rem(me + far, n)},
                device_id_type=MESH,
            )

        def sized(far, other, act):
            close = half(me) == half(other)
            pl.when(close)(lambda: act(copy(far, wide)))
            pl.when(jnp.logical_not(close))(lambda: act(copy(far, capacity)))

        for far in order:

            def pack(k, carry):
                packed[far - 1, k] = held_ref[picks_ref[(far - 1) * depth + k]]
                return carry

            lax.fori_loop(0, wide, pack, 0)
            sized(far, lax.rem(me + far, n), lambda one: one.start())
        for far in order:
            sized(far, lax.rem(me + far, n), lambda one: one.wait_send())
            sized(far, lax.rem(me - far + n, n), lambda one: one.wait_recv())

    for index, capacity in enumerate(capacities):
        pl.when(row == index)(functools.partial(exchange, capacity))


def picked_blocks(n, capacities, collective, picks, held):
    depth, block, cells = held.shape
    most = min(max(capacities) + EXTRA, depth)
    shape = (n - 1, most, block, cells)
    return pl.pallas_call(
        functools.partial(pick_kernel, n, capacities),
        out_shape=jax.ShapeDtypeStruct(shape, jnp.float32),
        in_specs=[
            pl.BlockSpec(memory_space=pltpu.SMEM),
            pl.BlockSpec(memory_space=pltpu.VMEM),
        ],
        out_specs=pl.BlockSpec(memory_space=pl.ANY),
        scratch_shapes=[
            pltpu.VMEM(shape, jnp.float32),
            pltpu.SemaphoreType.DMA((n - 1,)),
            pltpu.SemaphoreType.DMA((n - 1,)),
        ],
        compiler_params=pltpu.CompilerParams(
            collective_id=collective,
            has_side_effects=True,
            vmem_limit_bytes=24 * 1024 * 1024,
        ),
        cost_estimate=pl.CostEstimate(
            flops=0, bytes_accessed=4 * (n - 1) * most * block * cells * 4, transcendentals=0
        ),
    )(picks, held)


def slots_kernel(
    count_ref, cols_ref, dest_ref, rates_ref, near_ref, far_ref, factors_ref, theirs_ref, mine_ref
):
    basis = rates_ref.shape[1]
    depth = mine_ref.shape[0]
    near = near_ref.shape[0]
    theirs_ref[...] = jnp.zeros_like(theirs_ref)
    mine_ref[...] = jnp.zeros_like(mine_ref)

    def add_product(slot, block):
        weighted = jnp.concatenate(
            [(factors_ref[k : k + 1, :] * block).astype(jnp.bfloat16) for k in range(basis)], axis=0
        )
        rates = jnp.concatenate([rates_ref[slot, k] for k in range(basis)], axis=1)
        product = jnp.dot(rates, weighted, preferred_element_type=jnp.float32)
        place = dest_ref[slot]

        @pl.when(place < depth)
        def _():
            mine_ref[place] += product

        @pl.when(place >= depth)
        def _():
            theirs_ref[place - depth] += product

    def slot_step(slot, carry):
        column = cols_ref[slot]

        @pl.when(column < near)
        def _():
            add_product(slot, near_ref[column])

        @pl.when(column >= near)
        def _():
            add_product(slot, far_ref[column - near])

        return carry

    lax.fori_loop(0, count_ref[0], slot_step, 0)


def slot_sums(count, cols, dest, rates, near, far, factors):
    slots, basis, block, _ = rates.shape
    depth, _, cells = near.shape
    smem = pl.BlockSpec(memory_space=pltpu.SMEM)
    vmem = pl.BlockSpec(memory_space=pltpu.VMEM)
    half = jax.ShapeDtypeStruct((depth, block, cells), jnp.float32)
    return pl.pallas_call(
        slots_kernel,
        out_shape=(half, half),
        in_specs=[smem, smem, smem, vmem, vmem, vmem, vmem],
        out_specs=(vmem, vmem),
        compiler_params=pltpu.CompilerParams(vmem_limit_bytes=40 * 1024 * 1024),
        cost_estimate=pl.CostEstimate(
            flops=2 * slots * basis * block * block * cells,
            bytes_accessed=rates.size * 2 + far.size * 4 + 3 * depth * block * cells * 4,
            transcendentals=0,
        ),
    )(count, cols, dest, rates, near, far, factors)


def per_device(
    populations,
    source,
    loss_rates,
    basis_table,
    temp_bins,
    rate_blocks,
    block_rows,
    block_cols,
    block_count,
):
    levels, cells = populations.shape
    bin_count = basis_table.shape[1]
    block = rate_blocks.shape[-1]
    slots = rate_blocks.shape[2]
    per_piece = levels // block
    n = lax.axis_size("col")
    tile_rows = lax.axis_size("row")
    row, me = lax.axis_index("row"), lax.axis_index("col")
    onehot = (temp_bins[None, :] == jnp.arange(bin_count, dtype=jnp.int32)[:, None]).astype(
        jnp.float32
    )
    factors = jnp.dot(basis_table, onehot, precision=lax.Precision.HIGHEST)
    denominator = jnp.einsum("kl,kc->lc", loss_rates, factors, precision=lax.Precision.HIGHEST)
    denominator = denominator.reshape(per_piece, block, cells)
    source = source.reshape(per_piece, block, cells)
    rates = rate_blocks[0, 0]
    rows, cols, count = block_rows[0, 0], block_cols[0, 0], block_count[0]
    own = rows // per_piece == row
    dest = rows % per_piece + jnp.where(own, 0, per_piece)

    def sweeps(columns, gather):
        held = populations.reshape(per_piece, block, cells)
        for sweep in range(ITERS):
            theirs, mine = slot_sums(count, columns, dest, rates, held, gather(held), factors)
            arrived = lax.ppermute(theirs, "row", [(0, 1), (1, 0)])
            held = (source + (mine + arrived)) / denominator
        return held.reshape(levels, cells)

    def whole():
        return sweeps(
            cols + per_piece, lambda held: lax.all_gather(held, "col", axis=0, tiled=True)
        )

    pairs = []
    for high, low in CAPACITIES:
        if high < per_piece:
            pairs += [(high, low), (low, high)]
    if not pairs:
        return whole()

    live = jnp.arange(slots, dtype=jnp.int32) < count[0]
    spots = jnp.arange(n * per_piece, dtype=jnp.int32)
    named = jnp.any((cols[None, :] == spots[:, None]) & live[None, :], axis=1).astype(jnp.int32)
    every = lax.all_gather(named, ("row", "col"), axis=0)
    every = every.reshape(tile_rows, n, n, per_piece)
    line = jnp.arange(n, dtype=jnp.int32)
    same = (2 * line[:, None]) // n == (2 * line[None, :]) // n
    apart = line[:, None] != line[None, :]
    excess = jnp.where(same, EXTRA, 0).astype(jnp.int32)
    needed = jnp.max(
        jnp.where(apart[None], jnp.sum(every, axis=3) - excess[None], 0), axis=(1, 2)
    )

    ranks = jnp.arange(per_piece, dtype=jnp.int32)
    below = (ranks[:, None] < ranks[None, :]).astype(jnp.int32)

    def order(mask):
        return jnp.sum(mask[..., :, None] * below, axis=-2)

    asked = lax.dynamic_index_in_dim(
        lax.dynamic_index_in_dim(every, row, 0, False), me, 1, False
    )
    at = order(asked)
    chosen = (at[:, :, None] == ranks[None, None, :]) & (asked[:, :, None] > 0)
    lists = jnp.sum(jnp.where(chosen, ranks[None, :, None], 0), axis=1)
    readers = (me + jnp.arange(1, n, dtype=jnp.int32)) % n
    picks = jnp.sum(
        jnp.where((readers[:, None] == jnp.arange(n)[None, :])[:, :, None], lists[None], 0), axis=1
    ).reshape(-1)

    places = order(named.reshape(n, per_piece)).reshape(-1)
    place = jnp.sum(jnp.where(cols[None, :] == spots[:, None], places[:, None], 0), axis=0)
    back = (me - cols // per_piece + n) % n

    def sparse(index, capacities):
        most = min(max(capacities) + EXTRA, per_piece)
        columns = jnp.where(
            back == 0, cols % per_piece, per_piece + (back - 1) * most + place
        ).astype(jnp.int32)

        def gather(held):
            got = picked_blocks(n, capacities, index, picks, held)
            return got.reshape((n - 1) * most, block, cells)

        return lambda: sweeps(columns, gather)

    table = jnp.asarray(pairs + [(per_piece, per_piece)], jnp.int32)
    fits = jnp.all(needed[None, :] <= table, axis=1)
    branch = jnp.argmax(fits).astype(jnp.int32)
    return lax.switch(branch, [sparse(i, pair) for i, pair in enumerate(pairs)] + [whole])


def solution(mesh):
    in_specs = (
        P(("row", "col"), "cell"),
        P(("row", "col"), "cell"),
        P(None, ("row", "col")),
        P(),
        P("cell"),
        P("row", "col", None, None, None, None),
        P("row", "col", None),
        P("row", "col", None),
        P("row", "col"),
    )
    out_specs = P(("row", "col"), "cell")
    return jax.shard_map(
        per_device, mesh=mesh, in_specs=in_specs, out_specs=out_specs, check_vma=False
    )
```

```python
import functools

import jax
import jax.numpy as jnp
from jax import lax
from jax.experimental import pallas as pl
from jax.experimental.pallas import tpu as pltpu
from jax.sharding import PartitionSpec as P

ITERS = 2


MESH = pl.DeviceIdType.MESH
CAPACITIES = ((8, 4), (9, 5), (10, 5), (10, 6), (11, 6), (12, 8))
EXTRA = 1


def pick_kernel(n, capacities, picks_ref, held_ref, got_ref, packed, send_sem, recv_sem):
    me = lax.axis_index("col")
    row = lax.axis_index("row")
    depth = held_ref.shape[0]
    barrier = pltpu.get_barrier_semaphore()
    for far in range(1, n):
        peer = lax.rem(me + far, n)
        pl.semaphore_signal(barrier, inc=1, device_id={"col": peer}, device_id_type=MESH)
    pl.semaphore_wait(barrier, n - 1)

    def half(device):
        return lax.div(2 * device, n)

    def exchange(capacity):
        wide = min(capacity + EXTRA, depth)
        order = sorted(range(1, n), key=lambda far: abs(2 * far - n))

        def copy(far, size):
            return pltpu.make_async_remote_copy(
                src_ref=packed.at[far - 1, pl.ds(0, size)],
                dst_ref=got_ref.at[far - 1, pl.ds(0, size)],
                send_sem=send_sem.at[far - 1],
                recv_sem=recv_sem.at[far - 1],
                device_id={"col": lax.rem(me + far, n)},
                device_id_type=MESH,
            )

        def sized(far, other, act):
            close = half(me) == half(other)
            pl.when(close)(lambda: act(copy(far, wide)))
            pl.when(jnp.logical_not(close))(lambda: act(copy(far, capacity)))

        for far in order:

            def pack(k, carry):
                packed[far - 1, k] = held_ref[picks_ref[(far - 1) * depth + k]]
                return carry

            lax.fori_loop(0, wide, pack, 0)
            sized(far, lax.rem(me + far, n), lambda one: one.start())
        for far in order:
            sized(far, lax.rem(me + far, n), lambda one: one.wait_send())
            sized(far, lax.rem(me - far + n, n), lambda one: one.wait_recv())

    for index, capacity in enumerate(capacities):
        pl.when(row == index)(functools.partial(exchange, capacity))


def picked_blocks(n, capacities, collective, picks, held):
    depth, block, cells = held.shape
    most = min(max(capacities) + EXTRA, depth)
    shape = (n - 1, most, block, cells)
    return pl.pallas_call(
        functools.partial(pick_kernel, n, capacities),
        out_shape=jax.ShapeDtypeStruct(shape, jnp.float32),
        in_specs=[
            pl.BlockSpec(memory_space=pltpu.SMEM),
            pl.BlockSpec(memory_space=pltpu.VMEM),
        ],
        out_specs=pl.BlockSpec(memory_space=pl.ANY),
        scratch_shapes=[
            pltpu.VMEM(shape, jnp.float32),
            pltpu.SemaphoreType.DMA((n - 1,)),
            pltpu.SemaphoreType.DMA((n - 1,)),
        ],
        compiler_params=pltpu.CompilerParams(
            collective_id=collective,
            has_side_effects=True,
            vmem_limit_bytes=24 * 1024 * 1024,
        ),
        cost_estimate=pl.CostEstimate(
            flops=0, bytes_accessed=4 * (n - 1) * most * block * cells * 4, transcendentals=0
        ),
    )(picks, held)


def slots_kernel(
    count_ref, cols_ref, dest_ref, rates_ref, near_ref, far_ref, factors_ref, theirs_ref, mine_ref
):
    basis = rates_ref.shape[1]
    depth = mine_ref.shape[0]
    near = near_ref.shape[0]
    theirs_ref[...] = jnp.zeros_like(theirs_ref)
    mine_ref[...] = jnp.zeros_like(mine_ref)

    def add_product(slot, block):
        weighted = jnp.concatenate(
            [(factors_ref[k : k + 1, :] * block).astype(jnp.bfloat16) for k in range(basis)], axis=0
        )
        rates = jnp.concatenate([rates_ref[slot, k] for k in range(basis)], axis=1)
        product = jnp.dot(rates, weighted, preferred_element_type=jnp.float32)
        place = dest_ref[slot]

        @pl.when(place < depth)
        def _():
            mine_ref[place] += product

        @pl.when(place >= depth)
        def _():
            theirs_ref[place - depth] += product

    def slot_step(slot, carry):
        column = cols_ref[slot]

        @pl.when(column < near)
        def _():
            add_product(slot, near_ref[column])

        @pl.when(column >= near)
        def _():
            add_product(slot, far_ref[column - near])

        return carry

    lax.fori_loop(0, count_ref[0], slot_step, 0)


def slot_sums(count, cols, dest, rates, near, far, factors):
    slots, basis, block, _ = rates.shape
    depth, _, cells = near.shape
    smem = pl.BlockSpec(memory_space=pltpu.SMEM)
    vmem = pl.BlockSpec(memory_space=pltpu.VMEM)
    half = jax.ShapeDtypeStruct((depth, block, cells), jnp.float32)
    return pl.pallas_call(
        slots_kernel,
        out_shape=(half, half),
        in_specs=[smem, smem, smem, vmem, vmem, vmem, vmem],
        out_specs=(vmem, vmem),
        compiler_params=pltpu.CompilerParams(vmem_limit_bytes=40 * 1024 * 1024),
        cost_estimate=pl.CostEstimate(
            flops=2 * slots * basis * block * block * cells,
            bytes_accessed=rates.size * 2 + far.size * 4 + 3 * depth * block * cells * 4,
            transcendentals=0,
        ),
    )(count, cols, dest, rates, near, far, factors)


def per_device(
    populations,
    source,
    loss_rates,
    basis_table,
    temp_bins,
    rate_blocks,
    block_rows,
    block_cols,
    block_count,
):
    levels, cells = populations.shape
    bin_count = basis_table.shape[1]
    block = rate_blocks.shape[-1]
    slots = rate_blocks.shape[2]
    per_piece = levels // block
    n = lax.axis_size("col")
    tile_rows = lax.axis_size("row")
    row, me = lax.axis_index("row"), lax.axis_index("col")
    onehot = (temp_bins[None, :] == jnp.arange(bin_count, dtype=jnp.int32)[:, None]).astype(
        jnp.float32
    )
    factors = jnp.dot(basis_table, onehot, precision=lax.Precision.HIGHEST)
    denominator = jnp.einsum("kl,kc->lc", loss_rates, factors, precision=lax.Precision.HIGHEST)
    denominator = denominator.reshape(per_piece, block, cells)
    source = source.reshape(per_piece, block, cells)
    rates = rate_blocks[0, 0]
    rows, cols, count = block_rows[0, 0], block_cols[0, 0], block_count[0]
    own = rows // per_piece == row
    dest = rows % per_piece + jnp.where(own, 0, per_piece)

    def sweeps(columns, gather):
        held = populations.reshape(per_piece, block, cells)
        for sweep in range(ITERS):
            theirs, mine = slot_sums(count, columns, dest, rates, held, gather(held), factors)
            arrived = lax.ppermute(theirs, "row", [(0, 1), (1, 0)])
            held = (source + (mine + arrived)) / denominator
        return held.reshape(levels, cells)

    def whole():
        return sweeps(
            cols + per_piece, lambda held: lax.all_gather(held, "col", axis=0, tiled=True)
        )

    pairs = []
    for high, low in CAPACITIES:
        if high < per_piece:
            pairs += [(high, low), (low, high)]
    if not pairs:
        return whole()

    live = jnp.arange(slots, dtype=jnp.int32) < count[0]
    spots = jnp.arange(n * per_piece, dtype=jnp.int32)
    named = jnp.any((cols[None, :] == spots[:, None]) & live[None, :], axis=1).astype(jnp.int32)
    every = lax.all_gather(named, ("row", "col"), axis=0)
    every = every.reshape(tile_rows, n, n, per_piece)
    line = jnp.arange(n, dtype=jnp.int32)
    same = (2 * line[:, None]) // n == (2 * line[None, :]) // n
    apart = line[:, None] != line[None, :]
    excess = jnp.where(same, EXTRA, 0).astype(jnp.int32)
    needed = jnp.max(
        jnp.where(apart[None], jnp.sum(every, axis=3) - excess[None], 0), axis=(1, 2)
    )

    ranks = jnp.arange(per_piece, dtype=jnp.int32)
    below = (ranks[:, None] < ranks[None, :]).astype(jnp.int32)

    def order(mask):
        return jnp.sum(mask[..., :, None] * below, axis=-2)

    asked = lax.dynamic_index_in_dim(
        lax.dynamic_index_in_dim(every, row, 0, False), me, 1, False
    )
    at = order(asked)
    chosen = (at[:, :, None] == ranks[None, None, :]) & (asked[:, :, None] > 0)
    lists = jnp.sum(jnp.where(chosen, ranks[None, :, None], 0), axis=1)
    readers = (me + jnp.arange(1, n, dtype=jnp.int32)) % n
    picks = jnp.sum(
        jnp.where((readers[:, None] == jnp.arange(n)[None, :])[:, :, None], lists[None], 0), axis=1
    ).reshape(-1)

    places = order(named.reshape(n, per_piece)).reshape(-1)
    place = jnp.sum(jnp.where(cols[None, :] == spots[:, None], places[:, None], 0), axis=0)
    back = (me - cols // per_piece + n) % n

    def sparse(index, capacities):
        most = min(max(capacities) + EXTRA, per_piece)
        columns = jnp.where(
            back == 0, cols % per_piece, per_piece + (back - 1) * most + place
        ).astype(jnp.int32)

        def gather(held):
            got = picked_blocks(n, capacities, index, picks, held)
            return got.reshape((n - 1) * most, block, cells)

        return lambda: sweeps(columns, gather)

    table = jnp.asarray(pairs + [(per_piece, per_piece)], jnp.int32)
    fits = jnp.all(needed[None, :] <= table, axis=1)
    branch = jnp.argmax(fits).astype(jnp.int32)
    return lax.switch(branch, [sparse(i, pair) for i, pair in enumerate(pairs)] + [whole])


def solution(mesh):
    in_specs = (
        P(("row", "col"), "cell"),
        P(("row", "col"), "cell"),
        P(None, ("row", "col")),
        P(),
        P("cell"),
        P("row", "col", None, None, None, None),
        P("row", "col", None),
        P("row", "col", None),
        P("row", "col"),
    )
    out_specs = P(("row", "col"), "cell")
    return jax.shard_map(
        per_device, mesh=mesh, in_specs=in_specs, out_specs=out_specs, check_vma=False
    )
```
